512 devices in a mesh: ladder: 16 (over x, z_hi, core), space: 32 (over z_lo, y).
Axes of the slice: x: 4, y: 4, z: 16 (z_hi: 2, z_lo: 8; z = z_hi * 8 + z_lo), core: 2. Of those that a mesh axis runs over, the one named last changes fastest.
Arguments:
- initial: float32 [16, 1024, 2048], P('ladder', 'space'), may hold values from -1.2 to 1.2
- mobility: float32 [1024, 2048], P('space'), may hold values from 0.1 to 0.5
- tilt: float32 [1024, 2048], P('space'), may hold values from -0.5 to 0.5
- drift: float32 [2048], replicated, may hold values from -0.6 to 0.6
- mix_weights: float32 [16, 2], P('ladder'), may hold values from 0.2 to 0.4
Outputs:
- path: float32 [16, 1024, 2048], P('ladder', 'space')
The draws below stay inside these ranges and needn't reach their ends.
All inputs are finite; a program needn't handle non-finite values.
Results may differ from the reference program's by a relative error of at most 0.00002.
Values sent between devices are 32-bit elements; how exact they have to be, the bound alone decides.
No kernel may reach another device: no remote copies, remote signals or barrier semaphores. Data moves between devices by JAX's collectives and lax.ppermute only.
A program may use at most 64 MiB of HBM per device.

```python
import math
import jax
import jax.numpy as jnp

COLS = 2048
STEPS = 12
CYCLES = 2
IMAGES = 16
ROWS = 1024


def steps_of(rng, extent, cuts, smallest, largest):
    def one(axis_at, parts):
        heights = jax.random.uniform(jax.random.fold_in(jax.random.fold_in(rng, 6), axis_at), (parts,), jnp.float32, smallest / len(cuts), largest / len(cuts))
        return jnp.repeat(jnp.exp(heights), extent[axis_at] // parts).reshape((-1,) + (1,) * (len(extent) - axis_at - 1))

    loudness = one(*cuts[0])
    for cut in cuts[1:]:
        loudness = loudness * one(*cut)
    return loudness


def setup_inputs(seed: int = 0) -> dict:
    splits = jax.random.split(jax.random.key(seed), 6)
    initial = jnp.clip(jax.random.uniform(splits[0], (IMAGES, ROWS, COLS), jnp.float32, -1.2, 1.2) * steps_of(splits[0], (IMAGES, ROWS, COLS), ((0, 16), (1, 32)), -0.4, 0.0), -1.2, 1.2)
    mobility = jnp.clip(jnp.exp(math.log(0.5) - 1.609438 * jax.random.uniform(splits[1], (ROWS, COLS), jnp.float32) ** steps_of(splits[1], (ROWS, COLS), ((0, 32),), -0.2, 0.2)), 0.1, 0.5)
    tilt = jnp.clip(jax.random.uniform(splits[2], (ROWS, COLS), jnp.float32, -0.5, 0.5) * steps_of(splits[2], (ROWS, COLS), ((0, 32),), -0.4, 0.0), -0.5, 0.5)
    drift = jnp.clip(jax.random.uniform(splits[3], (COLS,), jnp.float32, -0.6, 0.6), -0.6, 0.6)
    mix_weights = jnp.clip(0.2 + 0.2 * jax.random.uniform(splits[4], (IMAGES, 2), jnp.float32) ** steps_of(splits[4], (IMAGES, 2), ((0, 16),), -0.2, 0.2), 0.2, 0.4)
    return dict(initial=initial, mobility=mobility, tilt=tilt, drift=drift, mix_weights=mix_weights)


def advance(field, mobility, tilt, rising, falling):
    below = jnp.roll(field, 1, -2)
    above = jnp.roll(field, -1, -2)
    vertical = below + above
    horizontal = jnp.roll(field, 1, -1) + jnp.roll(field, -1, -1)
    laplace = vertical + horizontal - 4.0 * field
    transport = rising * (field - below) + falling * (above - field)
    return field + 0.1 * mobility * (laplace + field - field * field * field + tilt) - transport


def reference(initial, mobility, tilt, drift, mix_weights):
    field = initial
    rising = jnp.maximum(drift, 0.0)[None, None, :]
    falling = jnp.minimum(drift, 0.0)[None, None, :]
    lower_w = mix_weights[:, 0][:, None, None]
    upper_w = mix_weights[:, 1][:, None, None]
    for cycle in range(CYCLES):
        for step in range(STEPS):
            field = advance(field, mobility[None], tilt[None], rising, falling)
        lower = jnp.concatenate([field[:1], field[:-1]], axis=0)
        upper = jnp.concatenate([field[1:], field[-1:]], axis=0)
        field = (1.0 - lower_w - upper_w) * field + lower_w * lower + upper_w * upper
    return field
```

```python
import functools

import jax
import jax.numpy as jnp
from jax import lax
from jax.experimental import pallas as pl
from jax.experimental.pallas import tpu as pltpu
from jax.sharding import PartitionSpec as P

DEPTH = 12
RIM = 2 * DEPTH
LANES = 128
SUB = 8
FIRST = 36


def spans(k, cycle, height):
    rim = RIM - DEPTH * cycle
    begin = FIRST - rim + k
    end = FIRST + height + rim - k
    return begin // SUB, -(-end // SUB)


def sweep(src, dst, mob, tilt, drift, span):
    planes = src.shape[0]
    lane = lax.broadcasted_iota(jnp.int32, (SUB, LANES), 1)
    is_first = lane == 0
    is_last = lane == LANES - 1
    for j in range(planes):
        u = jnp.broadcast_to(drift[j : j + 1, :], (SUB, LANES))
        rising = u > 0
        speed = jnp.abs(u)
        left = (j - 1) % planes
        right = (j + 1) % planes
        for i in range(*span):
            r = i * SUB
            f = src[j, r : r + SUB, :]
            below = src[j, r - 1 : r - 1 + SUB, :]
            above = src[j, r + 1 : r + 1 + SUB, :]
            west = pltpu.roll(jnp.where(is_last, src[left, r : r + SUB, :], f), 1, 1)
            east = pltpu.roll(jnp.where(is_first, src[right, r : r + SUB, :], f), LANES - 1, 1)
            near = (west + east) + (below + above)
            m = mob[j, r : r + SUB, :]
            t = tilt[j, r : r + SUB, :]
            gain = m * ((near + t) - f * (f * f + 3.0))
            dst[j, r : r + SUB, :] = (f + gain) + speed * (jnp.where(rising, below, above) - f)


def run_cycle(a, b, mob, tilt, drift, cycle, height):
    k = 1
    while k <= DEPTH:
        span = spans(k, cycle, height)
        last = k
        while last < DEPTH and spans(last + 1, cycle, height) == span:
            last += 1
        if k % 2 == 0:
            sweep(b, a, mob, tilt, drift, span)
            k += 1
            continue
        pairs = (last - k + 1) // 2
        if pairs:

            @pl.loop(0, pairs)
            def _(_):
                sweep(a, b, mob, tilt, drift, span)
                sweep(b, a, mob, tilt, drift, span)

            k += 2 * pairs
        else:
            sweep(a, b, mob, tilt, drift, span)
            k += 1


def place(dst, at, ref):
    for j in range(dst.shape[0]):
        for r in range(0, ref.shape[0], SUB):
            dst[j, at + r : at + r + SUB, :] = ref[r : r + SUB, j * LANES : (j + 1) * LANES]


def blank(ref, height):
    lo = FIRST - RIM
    hi = FIRST + height + RIM
    planes, rows, _ = ref.shape
    for j in range(planes):
        ref[j, 0:16, :] = jnp.zeros((16, LANES), jnp.float32)
        ref[j, rows - 16 : rows, :] = jnp.zeros((16, LANES), jnp.float32)


def own_kernel(u, lo, hi, mb, tl, clo, chi, drift, p, mob, tilt, a, b):
    height = u.shape[0]
    planes = a.shape[0]
    for ref in (a, b, mob, tilt):
        blank(ref, height)
    for k, (dst, src, scale) in enumerate(((mob, mb, 0.1), (tilt, tl, None))):
        for at, part in ((FIRST - RIM, clo.at[k]), (FIRST, src), (FIRST + height, chi.at[k])):
            for j in range(planes):
                for r in range(0, part.shape[0], SUB):
                    v = part[r : r + SUB, j * LANES : (j + 1) * LANES]
                    dst[j, at + r : at + r + SUB, :] = v if scale is None else v * scale
    place(a, FIRST - RIM, lo)
    place(a, FIRST, u)
    place(a, FIRST + height, hi)
    run_cycle(a, b, mob, tilt, drift, 0, height)
    p[...] = a[:, FIRST - DEPTH : FIRST + height + DEPTH, :]


def recv_kernel(u, lo, hi, mob, tilt, drift, p, a, b):
    height = u.shape[0]
    for ref in (a, b):
        blank(ref, height)
    place(a, FIRST - RIM, lo)
    place(a, FIRST, u)
    place(a, FIRST + height, hi)
    run_cycle(a, b, mob, tilt, drift, 0, height)
    p[...] = a[:, FIRST - DEPTH : FIRST + height + DEPTH, :]


def second_kernel(w, mid, one, two, mob, tilt, drift, q, a, b):
    planes, height, _ = q.shape
    for ref in (a, b):
        blank(ref, height)
    for j in range(planes):
        for r in range(0, mid.shape[1], SUB):
            at = FIRST - DEPTH + r
            a[j, at : at + SUB, :] = (
                w[0] * mid[j, r : r + SUB, :] + w[1] * one[j, r : r + SUB, :] + w[2] * two[j, r : r + SUB, :]
            )
    run_cycle(a, b, mob, tilt, drift, 1, height)
    q[...] = a[:, FIRST : FIRST + height, :]


def last_kernel(w, mid, one, two, out):
    for j in range(mid.shape[0]):
        for r in range(0, mid.shape[1], SUB):
            out[r : r + SUB, j * LANES : (j + 1) * LANES] = (
                w[0] * mid[j, r : r + SUB, :] + w[1] * one[j, r : r + SUB, :] + w[2] * two[j, r : r + SUB, :]
            )


VMEM = pl.BlockSpec(memory_space=pltpu.VMEM)
SMEM = pl.BlockSpec(memory_space=pltpu.SMEM)


def call(kernel, name, specs, shapes, scratch, ops):
    out = [jax.ShapeDtypeStruct(s, jnp.float32) for s in shapes]
    single = len(out) == 1
    return pl.pallas_call(
        kernel,
        out_shape=out[0] if single else out,
        in_specs=specs,
        out_specs=VMEM if single else [VMEM] * len(out),
        scratch_shapes=[pltpu.VMEM(s, jnp.float32) for s in scratch],
        compiler_params=pltpu.CompilerParams(vmem_limit_bytes=6 * 2**20),
        cost_estimate=pl.CostEstimate(flops=ops, bytes_accessed=2**20, transcendentals=0),
        name=name,
    )


def body(initial, mobility, tilt, drift, mix_weights):
    ladder = lax.axis_size("ladder")
    space = lax.axis_size("space")
    image = lax.axis_index("ladder")
    slab = lax.axis_index("space")
    height, cols = initial.shape[1:]
    planes = cols // LANES
    rows = height + 2 * RIM + 24
    work = (planes, rows, LANES)

    def off(i):
        return (i - 1) % ladder if i % 2 == 0 else (i + 1) % ladder

    def beyond(i):
        return (i - 3) % ladder if i % 2 == 0 else (i + 3) % ladder

    swap_off = [(i, off(i)) for i in range(ladder)]
    swap_on = [(i, i ^ 1) for i in range(ladder)]
    swap_beyond = [(i, beyond(i)) for i in range(ladder)]
    both = ("ladder", "space")
    rise = [
        (i * space + s, i * space + s + 1 if s < space - 1 else off(i) * space)
        for i in range(ladder)
        for s in range(space)
    ]
    fall = [(b, a) for a, b in rise]

    own = initial[0]
    other = lax.ppermute(own, "ladder", swap_off)
    coeffs = jnp.stack([mobility, tilt])
    c_lo = lax.ppermute(coeffs[:, height - RIM :], both, rise)
    c_hi = lax.ppermute(coeffs[:, :RIM], both, fall)
    own_lo = lax.ppermute(own[height - RIM :], "space", [(s, (s + 1) % space) for s in range(space)])
    own_hi = lax.ppermute(own[:RIM], "space", [((s + 1) % space, s) for s in range(space)])
    w_off = lax.ppermute(mix_weights, "ladder", swap_off)
    own_lo, w_off = lax.optimization_barrier((own_lo, w_off))
    w_off = w_off[0]
    w_own = mix_weights[0]
    flow = drift.reshape(planes, LANES)

    p_own, mob, til = call(
        own_kernel, "own_first", [VMEM] * 8, [(planes, height + 2 * DEPTH, LANES), work, work], [work, work], 10**8
    )(own, own_lo, own_hi, mobility, tilt, c_lo, c_hi, flow)
    p_on = lax.ppermute(p_own, "ladder", swap_on)

    top = jnp.where(slab == space - 1, own[height - RIM :], other[height - RIM :])
    bottom = jnp.where(slab == 0, own[:RIM], other[:RIM])
    off_lo = lax.ppermute(top, both, rise)
    off_hi = lax.ppermute(bottom, both, fall)
    p_off = call(
        recv_kernel, "off_first", [VMEM] * 6, [(planes, height + 2 * DEPTH, LANES)], [work, work], 10**8
    )(other, off_lo, off_hi, mob, til, flow)
    p_beyond = lax.ppermute(p_off, "ladder", swap_beyond)

    even = image % 2 == 0
    toward_off = jnp.where(even, w_own[0], w_own[1])
    toward_on = jnp.where(even, w_own[1], w_own[0])
    rest = 1.0 - w_own[0] - w_own[1]
    at_end = (image == 0) | (image == ladder - 1)
    w_mine = jnp.stack([jnp.where(at_end, rest + toward_off, rest), jnp.where(at_end, 0.0, toward_off), toward_on])
    back = jnp.where(even, w_off[1], w_off[0])
    on = jnp.where(even, w_off[0], w_off[1])
    w_theirs = jnp.stack([1.0 - w_off[0] - w_off[1], back, on])

    second = call(
        second_kernel, "second", [SMEM] + [VMEM] * 6, [(planes, height, LANES)], [work, work], 10**8
    )
    q_own = second(w_mine, p_own, p_off, p_on, mob, til, flow)
    q_on = lax.ppermute(q_own, "ladder", swap_on)
    q_off = second(w_theirs, p_off, p_own, p_beyond, mob, til, flow)
    path = call(last_kernel, "blend", [SMEM] + [VMEM] * 3, [(height, cols)], [], 10**6)(w_mine, q_own, q_off, q_on)
    return path[None]


def solution(mesh):
    in_specs = (
        P("ladder", "space", None),
        P("space", None),
        P("space", None),
        P(),
        P("ladder", None),
    )
    out_specs = P("ladder", "space", None)
    return jax.shard_map(body, mesh=mesh, in_specs=in_specs, out_specs=out_specs, check_vma=False)
```

```python
import functools

import jax
import jax.numpy as jnp
from jax import lax
from jax.experimental import pallas as pl
from jax.experimental.pallas import tpu as pltpu
from jax.sharding import PartitionSpec as P

DEPTH = 12
RIM = 2 * DEPTH
LANES = 128
SUB = 8
FIRST = 36


def spans(k, cycle, height):
    rim = RIM - DEPTH * cycle
    begin = FIRST - rim + k
    end = FIRST + height + rim - k
    return begin // SUB, -(-end // SUB)


def sweep(src, dst, mob, tilt, drift, span):
    planes = src.shape[0]
    lane = lax.broadcasted_iota(jnp.int32, (SUB, LANES), 1)
    is_first = lane == 0
    is_last = lane == LANES - 1
    for j in range(planes):
        u = jnp.broadcast_to(drift[j : j + 1, :], (SUB, LANES))
        rising = u > 0
        speed = jnp.abs(u)
        left = (j - 1) % planes
        right = (j + 1) % planes
        for i in range(*span):
            r = i * SUB
            f = src[j, r : r + SUB, :]
            below = src[j, r - 1 : r - 1 + SUB, :]
            above = src[j, r + 1 : r + 1 + SUB, :]
            west = pltpu.roll(jnp.where(is_last, src[left, r : r + SUB, :], f), 1, 1)
            east = pltpu.roll(jnp.where(is_first, src[right, r : r + SUB, :], f), LANES - 1, 1)
            near = (west + east) + (below + above)
            m = mob[j, r : r + SUB, :]
            t = tilt[j, r : r + SUB, :]
            gain = m * ((near + t) - f * (f * f + 3.0))
            dst[j, r : r + SUB, :] = (f + gain) + speed * (jnp.where(rising, below, above) - f)


def run_cycle(a, b, mob, tilt, drift, cycle, height):
    k = 1
    while k <= DEPTH:
        span = spans(k, cycle, height)
        last = k
        while last < DEPTH and spans(last + 1, cycle, height) == span:
            last += 1
        if k % 2 == 0:
            sweep(b, a, mob, tilt, drift, span)
            k += 1
            continue
        pairs = (last - k + 1) // 2
        if pairs:

            @pl.loop(0, pairs)
            def _(_):
                sweep(a, b, mob, tilt, drift, span)
                sweep(b, a, mob, tilt, drift, span)

            k += 2 * pairs
        else:
            sweep(a, b, mob, tilt, drift, span)
            k += 1


def place(dst, at, tiles, first, count):
    planes = dst.shape[0]
    for j in range(planes):
        for i in range(count):
            r = at + i * SUB
            dst[j, r : r + SUB, :] = tiles[(first + i) * planes + j]


def blank(ref):
    planes, rows, _ = ref.shape
    for j in range(planes):
        ref[j, 0:16, :] = jnp.zeros((16, LANES), jnp.float32)
        ref[j, rows - 16 : rows, :] = jnp.zeros((16, LANES), jnp.float32)


def edges_kernel(msg, mobility, tilt, up, down, wrap):
    low_end = lax.axis_index("space") == 0
    planes = mobility.shape[1] // LANES
    tiles = mobility.shape[0] // SUB
    count = RIM // SUB
    skip = tiles - count
    for i in range(count):
        for j in range(planes):
            k = i * planes + j
            top = msg[k + skip * planes]
            bottom = msg[k]
            wrap[k] = jnp.where(low_end, bottom, top)
            lanes = slice(j * LANES, (j + 1) * LANES)
            lo = slice(i * SUB, (i + 1) * SUB)
            hi = slice((i + skip) * SUB, (i + skip + 1) * SUB)
            up[0, k] = top
            up[1, k] = mobility[hi, lanes]
            up[2, k] = tilt[hi, lanes]
            down[0, k] = bottom
            down[1, k] = mobility[lo, lanes]
            down[2, k] = tilt[lo, lanes]


def off_edges_kernel(msg, other, up, down):
    slab = lax.axis_index("space")
    low_end = slab == 0
    high_end = slab == lax.axis_size("space") - 1
    count = up.shape[0]
    skip = other.shape[0] - 1 - count
    for k in range(count):
        up[k] = jnp.where(high_end, msg[k + skip], other[k + skip])
        down[k] = jnp.where(low_end, msg[k], other[k])


def own_kernel(msg, lo, hi, wrap, mobility, tilt, drift, p, mob, til, a, b):
    slab = lax.axis_index("space")
    low_end = slab == 0
    high_end = slab == lax.axis_size("space") - 1
    height = mobility.shape[0]
    planes = a.shape[0]
    count = RIM // SUB
    for ref in (a, b, mob, til):
        blank(ref)
    for j in range(planes):
        for i in range(count):
            k = i * planes + j
            for at, got in ((FIRST - RIM, lo), (FIRST + height, hi)):
                r = at + i * SUB
                mob[j, r : r + SUB, :] = 0.1 * got[1, k]
                til[j, r : r + SUB, :] = got[2, k]
            r = FIRST - RIM + i * SUB
            a[j, r : r + SUB, :] = jnp.where(low_end, wrap[k], lo[0, k])
            r = FIRST + height + i * SUB
            a[j, r : r + SUB, :] = jnp.where(high_end, wrap[k], hi[0, k])
        for i in range(height // SUB):
            r = FIRST + i * SUB
            rows = slice(i * SUB, (i + 1) * SUB)
            lanes = slice(j * LANES, (j + 1) * LANES)
            mob[j, r : r + SUB, :] = 0.1 * mobility[rows, lanes]
            til[j, r : r + SUB, :] = tilt[rows, lanes]
    place(a, FIRST, msg, 0, height // SUB)
    run_cycle(a, b, mob, til, drift, 0, height)
    p[...] = a[:, FIRST - DEPTH : FIRST + height + DEPTH, :]


def off_kernel(msg, lo, hi, mob, til, drift, p, a, b):
    planes = a.shape[0]
    tiles = msg.shape[0] // planes
    height = tiles * SUB
    for ref in (a, b):
        blank(ref)
    place(a, FIRST - RIM, lo, 0, RIM // SUB)
    place(a, FIRST, msg, 0, tiles)
    place(a, FIRST + height, hi, 0, RIM // SUB)
    run_cycle(a, b, mob, til, drift, 0, height)
    p[...] = a[:, FIRST - DEPTH : FIRST + height + DEPTH, :]


def weights(msg):
    tile = msg[msg.shape[0] - 1]
    half = SUB // 2
    return jnp.broadcast_to(tile[0:1, :], tile.shape), jnp.broadcast_to(tile[half : half + 1, :], tile.shape)


def own_weights(msg):
    image = lax.axis_index("ladder")
    even = image % 2 == 0
    at_end = (image == 0) | (image == lax.axis_size("ladder") - 1)
    lower, upper = weights(msg)
    off = jnp.where(even, lower, upper)
    on = jnp.where(even, upper, lower)
    rest = 1.0 - lower - upper
    return jnp.where(at_end, rest + off, rest), jnp.where(at_end, 0.0, off), on


def off_weights(msg):
    even = lax.axis_index("ladder") % 2 == 0
    lower, upper = weights(msg)
    return 1.0 - lower - upper, jnp.where(even, upper, lower), jnp.where(even, lower, upper)


def second_kernel(which, msg, mid, one, two, mob, til, drift, q, a, b):
    planes, height, _ = q.shape
    for ref in (a, b):
        blank(ref)
    w = which(msg)
    for j in range(planes):
        for r in range(0, mid.shape[1], SUB):
            at = FIRST - DEPTH + r
            rows = slice(r, r + SUB)
            a[j, at : at + SUB, :] = w[0] * mid[j, rows, :] + w[1] * one[j, rows, :] + w[2] * two[j, rows, :]
    run_cycle(a, b, mob, til, drift, 1, height)
    q[...] = a[:, FIRST : FIRST + height, :]


def blend_kernel(msg, mid, one, two, out):
    w = own_weights(msg)
    for j in range(mid.shape[0]):
        for r in range(0, mid.shape[1], SUB):
            rows = slice(r, r + SUB)
            out[rows, j * LANES : (j + 1) * LANES] = (
                w[0] * mid[j, rows, :] + w[1] * one[j, rows, :] + w[2] * two[j, rows, :]
            )


VMEM = pl.BlockSpec(memory_space=pltpu.VMEM)


def call(kernel, name, operands, shapes, scratch=(), ops=10**3):
    out = [jax.ShapeDtypeStruct(s, jnp.float32) for s in shapes]
    single = len(out) == 1
    return pl.pallas_call(
        kernel,
        out_shape=out[0] if single else out,
        in_specs=[VMEM] * len(operands),
        out_specs=VMEM if single else [VMEM] * len(out),
        scratch_shapes=[pltpu.VMEM(s, jnp.float32) for s in scratch],
        compiler_params=pltpu.CompilerParams(vmem_limit_bytes=6 * 2**20),
        cost_estimate=pl.CostEstimate(flops=ops, bytes_accessed=2**10, transcendentals=0),
        name=name,
    )(*operands)


def body(initial, mobility, tilt, drift, mix_weights):
    ladder = lax.axis_size("ladder")
    space = lax.axis_size("space")
    height, cols = initial.shape[1:]
    planes = cols // LANES
    work = (planes, height + 2 * RIM + 24, LANES)
    wide = (planes, height + 2 * DEPTH, LANES)
    slab = (planes, height, LANES)
    rim = (planes * RIM // SUB, SUB, LANES)

    def off(i):
        return (i - 1) % ladder if i % 2 == 0 else (i + 1) % ladder

    def beyond(i):
        return (i - 3) % ladder if i % 2 == 0 else (i + 3) % ladder

    swap_off = [(i, off(i)) for i in range(ladder)]
    swap_on = [(i, i ^ 1) for i in range(ladder)]
    swap_beyond = [(i, beyond(i)) for i in range(ladder)]
    swap_ends = [(0, space - 1), (space - 1, 0)]
    both = ("ladder", "space")
    rise = [
        (i * space + s, i * space + s + 1 if s < space - 1 else off(i) * space)
        for i in range(ladder)
        for s in range(space)
    ]
    fall = [(b, a) for a, b in rise]

    half = SUB // 2
    tiles = initial.reshape(height // SUB, SUB, planes, LANES).transpose(0, 2, 1, 3).reshape(-1, SUB, LANES)
    pair = jnp.broadcast_to(mix_weights.reshape(2, 1, 1), (2, half, LANES)).reshape(1, SUB, LANES)
    msg = jnp.concatenate([tiles, pair])
    other = lax.ppermute(msg, "ladder", swap_off)
    flow = drift.reshape(planes, LANES)

    up, down, wrap = call(edges_kernel, "edges", (msg, mobility, tilt), [(3, *rim), (3, *rim), rim])
    wrap = lax.ppermute(wrap, "space", swap_ends)
    lo = lax.ppermute(up, both, rise)
    hi = lax.ppermute(down, both, fall)
    p_own, mob, til = call(
        own_kernel,
        "own_first",
        (msg, lo, hi, wrap, mobility, tilt, flow),
        [wide, work, work],
        [work, work],
    )
    p_own, other = lax.optimization_barrier((p_own, other))
    up, down = call(off_edges_kernel, "off_edges", (msg, other), [rim] * 2)
    p_own, up, down = lax.optimization_barrier((p_own, up, down))
    lo = lax.ppermute(up, both, rise)
    hi = lax.ppermute(down, both, fall)
    p_on = lax.ppermute(p_own, "ladder", swap_on)
    p_off = call(off_kernel, "off_first", (other, lo, hi, mob, til, flow), [wide], [work, work])
    p_beyond = lax.ppermute(p_off, "ladder", swap_beyond)

    q_own = call(
        functools.partial(second_kernel, own_weights),
        "own_second",
        (msg, p_own, p_off, p_on, mob, til, flow),
        [slab],
        [work, work],
        10**8,
    )
    q_on = lax.ppermute(q_own, "ladder", swap_on)
    q_off = call(
        functools.partial(second_kernel, off_weights),
        "off_second",
        (other, p_off, p_own, p_beyond, mob, til, flow),
        [slab],
        [work, work],
        10**8,
    )
    path = call(blend_kernel, "blend", (msg, q_own, q_off, q_on), [(height, cols)])
    return path[None]


def solution(mesh):
    in_specs = (
        P("ladder", "space", None),
        P("space", None),
        P("space", None),
        P(),
        P("ladder", None),
    )
    out_specs = P("ladder", "space", None)
    return jax.shard_map(body, mesh=mesh, in_specs=in_specs, out_specs=out_specs, check_vma=False)
```

```python
import functools

import jax
import jax.numpy as jnp
from jax import lax
from jax.experimental import pallas as pl
from jax.experimental.pallas import tpu as pltpu
from jax.sharding import PartitionSpec as P

DEPTH = 12
RIM = 2 * DEPTH
LANES = 128
SUB = 8
FIRST = 36


def spans(k, begin, end):
    return (begin + k) // SUB, -(-(end - k) // SUB)


def sweep(src, dst, mob, tilt, drift, span):
    planes = src.shape[0]
    lane = lax.broadcasted_iota(jnp.int32, (SUB, LANES), 1)
    is_first = lane == 0
    is_last = lane == LANES - 1
    for j in range(planes):
        u = jnp.broadcast_to(drift[j : j + 1, :], (SUB, LANES))
        rising = u > 0
        speed = jnp.abs(u)
        left = (j - 1) % planes
        right = (j + 1) % planes
        for i in range(*span):
            r = i * SUB
            f = src[j, r : r + SUB, :]
            below = src[j, r - 1 : r - 1 + SUB, :]
            above = src[j, r + 1 : r + 1 + SUB, :]
            west = pltpu.roll(jnp.where(is_last, src[left, r : r + SUB, :], f), 1, 1)
            east = pltpu.roll(jnp.where(is_first, src[right, r : r + SUB, :], f), LANES - 1, 1)
            near = (west + east) + (below + above)
            m = mob[j, r : r + SUB, :]
            t = tilt[j, r : r + SUB, :]
            gain = m * ((near + t) - f * (f * f + 3.0))
            dst[j, r : r + SUB, :] = (f + gain) + speed * (jnp.where(rising, below, above) - f)


def run_cycle(a, b, mob, tilt, drift, begin, end):
    k = 1
    while k <= DEPTH:
        span = spans(k, begin, end)
        last = k
        while last < DEPTH and spans(last + 1, begin, end) == span:
            last += 1
        if k % 2 == 0:
            sweep(b, a, mob, tilt, drift, span)
            k += 1
            continue
        pairs = (last - k + 1) // 2
        if pairs:

            @pl.loop(0, pairs)
            def _(_):
                sweep(a, b, mob, tilt, drift, span)
                sweep(b, a, mob, tilt, drift, span)

            k += 2 * pairs
        else:
            sweep(a, b, mob, tilt, drift, span)
            k += 1


def place(dst, at, tiles, first, count):
    planes = dst.shape[0]
    for j in range(planes):
        for i in range(count):
            r = at + i * SUB
            dst[j, r : r + SUB, :] = tiles[(first + i) * planes + j]


def blank(ref):
    planes, rows, _ = ref.shape
    for j in range(planes):
        ref[j, 0:16, :] = jnp.zeros((16, LANES), jnp.float32)
        ref[j, rows - 16 : rows, :] = jnp.zeros((16, LANES), jnp.float32)


def edges_kernel(msg, mobility, tilt, down, up):
    planes = mobility.shape[1] // LANES
    tiles = mobility.shape[0] // SUB
    count = RIM // SUB
    skip = tiles - count
    for i in range(count):
        for j in range(planes):
            k = i * planes + j
            lanes = slice(j * LANES, (j + 1) * LANES)
            lo = slice(i * SUB, (i + 1) * SUB)
            hi = slice((i + skip) * SUB, (i + skip + 1) * SUB)
            up[0, k] = msg[k + skip * planes]
            up[1, k] = mobility[hi, lanes]
            up[2, k] = tilt[hi, lanes]
            down[0, k] = msg[k]
            down[1, k] = mobility[lo, lanes]
            down[2, k] = tilt[lo, lanes]


def off_edges_kernel(msg, other, down, up, ends):
    slab = lax.axis_index("space")
    low_end = slab == 0
    high_end = slab == lax.axis_size("space") - 1
    count = up.shape[0]
    skip = other.shape[0] - 1 - count
    for k in range(count):
        top = other[k + skip]
        bottom = other[k]
        up[k] = jnp.where(high_end, msg[k + skip], top)
        down[k] = jnp.where(low_end, msg[k], bottom)
        ends[k] = jnp.where(low_end, bottom, top)


def own_kernel(msg, hi, lo, ends, mobility, tilt, drift, p, mob, til, a, b):
    slab = lax.axis_index("space")
    low_end = slab == 0
    high_end = slab == lax.axis_size("space") - 1
    height = mobility.shape[0]
    planes = a.shape[0]
    count = RIM // SUB
    for ref in (a, b, mob, til):
        blank(ref)
    for j in range(planes):
        for i in range(count):
            k = i * planes + j
            for at, got, alone in ((FIRST - RIM, lo, low_end), (FIRST + height, hi, high_end)):
                rows = slice(at + i * SUB, at + (i + 1) * SUB)
                a[j, rows, :] = jnp.where(alone, ends[k], got[0, k])
                mob[j, rows, :] = 0.1 * got[1, k]
                til[j, rows, :] = got[2, k]
        for i in range(height // SUB):
            at = FIRST + i * SUB
            rows = slice(i * SUB, (i + 1) * SUB)
            lanes = slice(j * LANES, (j + 1) * LANES)
            mob[j, at : at + SUB, :] = 0.1 * mobility[rows, lanes]
            til[j, at : at + SUB, :] = tilt[rows, lanes]
    place(a, FIRST, msg, 0, height // SUB)
    run_cycle(a, b, mob, til, drift, FIRST - RIM, FIRST + height + RIM)
    p[...] = a[:, FIRST - DEPTH : FIRST + height + DEPTH, :]


def off_kernel(msg, hi, lo, mob, til, drift, p, a, b):
    planes = a.shape[0]
    tiles = msg.shape[0] // planes
    height = tiles * SUB
    for ref in (a, b):
        blank(ref)
    place(a, FIRST - RIM, lo, 0, RIM // SUB)
    place(a, FIRST, msg, 0, tiles)
    place(a, FIRST + height, hi, 0, RIM // SUB)
    run_cycle(a, b, mob, til, drift, FIRST - RIM, FIRST + height + RIM)
    p[...] = a[:, FIRST - DEPTH : FIRST + height + DEPTH, :]


def weights(msg):
    tile = msg[msg.shape[0] - 1]
    half = SUB // 2
    return jnp.broadcast_to(tile[0:1, :], tile.shape), jnp.broadcast_to(tile[half : half + 1, :], tile.shape)


def own_weights(msg):
    image = lax.axis_index("ladder")
    even = image % 2 == 0
    at_end = (image == 0) | (image == lax.axis_size("ladder") - 1)
    lower, upper = weights(msg)
    off = jnp.where(even, lower, upper)
    on = jnp.where(even, upper, lower)
    rest = 1.0 - lower - upper
    return jnp.where(at_end, rest + off, rest), jnp.where(at_end, 0.0, off), on


def off_weights(msg):
    even = lax.axis_index("ladder") % 2 == 0
    lower, upper = weights(msg)
    return 1.0 - lower - upper, jnp.where(even, upper, lower), jnp.where(even, lower, upper)


def second_kernel(which, msg, mid, one, two, mob, til, drift, q, a, b):
    planes, height, _ = q.shape
    for ref in (a, b):
        blank(ref)
    w = which(msg)
    for j in range(planes):
        for r in range(0, mid.shape[1], SUB):
            at = FIRST - DEPTH + r
            rows = slice(r, r + SUB)
            a[j, at : at + SUB, :] = w[0] * mid[j, rows, :] + w[1] * one[j, rows, :] + w[2] * two[j, rows, :]
    run_cycle(a, b, mob, til, drift, FIRST - DEPTH, FIRST + height + DEPTH)
    q[...] = a[:, FIRST : FIRST + height, :]


def blend_kernel(msg, mid, one, two, out):
    w = own_weights(msg)
    for j in range(mid.shape[0]):
        for r in range(0, mid.shape[1], SUB):
            rows = slice(r, r + SUB)
            out[rows, j * LANES : (j + 1) * LANES] = (
                w[0] * mid[j, rows, :] + w[1] * one[j, rows, :] + w[2] * two[j, rows, :]
            )


VMEM = pl.BlockSpec(memory_space=pltpu.VMEM)


def call(kernel, name, operands, shapes, scratch=(), ops=10**3):
    out = [jax.ShapeDtypeStruct(s, jnp.float32) for s in shapes]
    single = len(out) == 1
    return pl.pallas_call(
        kernel,
        out_shape=out[0] if single else out,
        in_specs=[VMEM] * len(operands),
        out_specs=VMEM if single else [VMEM] * len(out),
        scratch_shapes=[pltpu.VMEM(s, jnp.float32) for s in scratch],
        compiler_params=pltpu.CompilerParams(vmem_limit_bytes=6 * 2**20),
        cost_estimate=pl.CostEstimate(flops=ops, bytes_accessed=2**10, transcendentals=0),
        name=name,
    )(*operands)


def body(initial, mobility, tilt, drift, mix_weights):
    ladder = lax.axis_size("ladder")
    space = lax.axis_size("space")
    height, cols = initial.shape[1:]
    planes = cols // LANES
    work = (planes, height + 2 * RIM + 24, LANES)
    wide = (planes, height + 2 * DEPTH, LANES)
    slab = (planes, height, LANES)
    rim = (planes * RIM // SUB, SUB, LANES)

    def off(i):
        return (i - 1) % ladder if i % 2 == 0 else (i + 1) % ladder

    def beyond(i):
        return (i - 3) % ladder if i % 2 == 0 else (i + 3) % ladder

    swap_off = [(i, off(i)) for i in range(ladder)]
    swap_on = [(i, i ^ 1) for i in range(ladder)]
    swap_beyond = [(i, beyond(i)) for i in range(ladder)]
    both = ("ladder", "space")
    rise = [
        (i * space + s, i * space + s + 1 if s < space - 1 else off(i) * space)
        for i in range(ladder)
        for s in range(space)
    ]
    fall = [(b, a) for a, b in rise]
    at_ends = [(i * space + s, off(i) * space + space - 1 - s) for i in range(ladder) for s in (0, space - 1)]

    half = SUB // 2
    tiles = initial.reshape(height // SUB, SUB, planes, LANES).transpose(0, 2, 1, 3).reshape(-1, SUB, LANES)
    pair = jnp.broadcast_to(mix_weights.reshape(2, 1, 1), (2, half, LANES)).reshape(1, SUB, LANES)
    msg = jnp.concatenate([tiles, pair])
    other = lax.ppermute(msg, "ladder", swap_off)
    flow = drift.reshape(planes, LANES)

    down, up = call(edges_kernel, "edges", (msg, mobility, tilt), [(3, *rim)] * 2)
    own_hi = lax.ppermute(down, both, fall)
    own_lo = lax.ppermute(up, both, rise)
    down, up, ends = call(off_edges_kernel, "off_edges", (msg, other), [rim] * 3, ops=4 * 10**10)
    hi = lax.ppermute(down, both, fall)
    lo = lax.ppermute(up, both, rise)
    ends = lax.ppermute(ends, both, at_ends)
    p_own, mob, til = call(
        own_kernel,
        "own_first",
        (msg, own_hi, own_lo, ends, mobility, tilt, flow),
        [wide, work, work],
        [work, work],
        5 * 10**9,
    )
    p_on = lax.ppermute(p_own, "ladder", swap_on)
    p_off = call(off_kernel, "off_first", (other, hi, lo, mob, til, flow), [wide], [work, work], 5 * 10**9)
    p_beyond = lax.ppermute(p_off, "ladder", swap_beyond)

    q_own = call(
        functools.partial(second_kernel, own_weights),
        "own_second",
        (msg, p_own, p_off, p_on, mob, til, flow),
        [slab],
        [work, work],
        4 * 10**9,
    )
    q_on = lax.ppermute(q_own, "ladder", swap_on)
    q_off = call(
        functools.partial(second_kernel, off_weights),
        "off_second",
        (other, p_off, p_own, p_beyond, mob, til, flow),
        [slab],
        [work, work],
        4 * 10**9,
    )
    path = call(blend_kernel, "blend", (msg, q_own, q_off, q_on), [(height, cols)])
    return path[None]


def solution(mesh):
    in_specs = (
        P("ladder", "space", None),
        P("space", None),
        P("space", None),
        P(),
        P("ladder", None),
    )
    out_specs = P("ladder", "space", None)
    return jax.shard_map(body, mesh=mesh, in_specs=in_specs, out_specs=out_specs, check_vma=False)
```

```python
import functools

import jax
import jax.numpy as jnp
from jax import lax
from jax.experimental import pallas as pl
from jax.experimental.pallas import tpu as pltpu
from jax.sharding import PartitionSpec as P

DEPTH = 12
RIM = 2 * DEPTH
LANES = 128
SUB = 8
GROUP = 4
FIRST = 36


def spans(k, begin, end):
    return (begin + k) // SUB, -(-(end - k) // SUB)


def sweep(src, dst, mob, tilt, drift, span):
    planes = src.shape[0]
    lane = lax.broadcasted_iota(jnp.int32, (SUB, LANES), 1)
    is_first = lane == 0
    is_last = lane == LANES - 1
    for begin in range(0, planes, GROUP):
        group = range(begin, begin + GROUP)
        drifts = [jnp.broadcast_to(drift[j : j + 1, :], (SUB, LANES)) for j in group]
        rising = [u > 0 for u in drifts]
        speed = [jnp.abs(u) for u in drifts]
        for i in range(*span):
            r = i * SUB
            fields = [src[(begin - 1 + n) % planes, r : r + SUB, :] for n in range(GROUP + 2)]
            for n, j in enumerate(group):
                f = fields[n + 1]
                below = src[j, r - 1 : r - 1 + SUB, :]
                above = src[j, r + 1 : r + 1 + SUB, :]
                west = pltpu.roll(jnp.where(is_last, fields[n], f), 1, 1)
                east = pltpu.roll(jnp.where(is_first, fields[n + 2], f), LANES - 1, 1)
                near = (west + east) + (below + above)
                m = mob[j, r : r + SUB, :]
                t = tilt[j, r : r + SUB, :]
                gain = m * ((near + t) - f * (f * f + 3.0))
                dst[j, r : r + SUB, :] = (f + gain) + speed[n] * (jnp.where(rising[n], below, above) - f)


def run_cycle(a, b, mob, tilt, drift, begin, end):
    k = 1
    while k <= DEPTH:
        span = spans(k, begin, end)
        last = k
        while last < DEPTH and spans(last + 1, begin, end) == span:
            last += 1
        if k % 2 == 0:
            sweep(b, a, mob, tilt, drift, span)
            k += 1
            continue
        pairs = (last - k + 1) // 2
        if pairs:

            @pl.loop(0, pairs)
            def _(_):
                sweep(a, b, mob, tilt, drift, span)
                sweep(b, a, mob, tilt, drift, span)

            k += 2 * pairs
        else:
            sweep(a, b, mob, tilt, drift, span)
            k += 1


def place(dst, at, tiles, first, count):
    planes = dst.shape[0]
    for j in range(planes):
        for i in range(count):
            r = at + i * SUB
            dst[j, r : r + SUB, :] = tiles[(first + i) * planes + j]


def blank(ref):
    planes, rows, _ = ref.shape
    for j in range(planes):
        ref[j, 0:16, :] = jnp.zeros((16, LANES), jnp.float32)
        ref[j, rows - 16 : rows, :] = jnp.zeros((16, LANES), jnp.float32)


def edges_kernel(msg, mobility, tilt, one, two):
    odd = lax.axis_index("space") % 2 == 1
    even = lax.axis_index("ladder") % 2 == 0
    planes = mobility.shape[1] // LANES
    tiles = mobility.shape[0] // SUB
    count = RIM // SUB
    skip = tiles - count
    for i in range(count):
        for j in range(planes):
            k = i * planes + j
            lanes = slice(j * LANES, (j + 1) * LANES)
            lo = slice(i * SUB, (i + 1) * SUB)
            hi = slice((i + skip) * SUB, (i + skip + 1) * SUB)
            tops = msg[k + skip * planes], jnp.where(even, mobility[hi, lanes], tilt[hi, lanes])
            bottoms = msg[k], jnp.where(even, mobility[lo, lanes], tilt[lo, lanes])
            for n in range(2):
                one[n, k] = jnp.where(odd, tops[n], bottoms[n])
                two[n, k] = jnp.where(odd, bottoms[n], tops[n])


def off_edges_kernel(other, one, two):
    odd = lax.axis_index("space") % 2 == 1
    count = one.shape[0]
    skip = other.shape[0] - 1 - count
    for k in range(count):
        top = other[k + skip]
        bottom = other[k]
        one[k] = jnp.where(odd, top, bottom)
        two[k] = jnp.where(odd, bottom, top)


def own_kernel(msg, one, two, on_one, on_two, off_one, mobility, tilt, drift, p, mob, til, a, b):
    slab = lax.axis_index("space")
    low_end = slab == 0
    high_end = slab == lax.axis_size("space") - 1
    even = lax.axis_index("ladder") % 2 == 0
    odd = slab % 2 == 1
    height = mobility.shape[0]
    planes = a.shape[0]
    count = RIM // SUB
    for ref in (a, b, mob, til):
        blank(ref)
    for j in range(planes):
        for i in range(count):
            k = i * planes + j
            got = [(one[n, k], two[n, k]) for n in range(2)] + [(on_one[k], on_two[k])]
            lo = [jnp.where(odd, y, x) for x, y in got]
            hi = [jnp.where(odd, x, y) for x, y in got]
            for at, g, alone in ((FIRST - RIM, lo, low_end), (FIRST + height, hi, high_end)):
                rows = slice(at + i * SUB, at + (i + 1) * SUB)
                a[j, rows, :] = jnp.where(alone, off_one[k], g[0])
                straight = even != alone
                mob[j, rows, :] = 0.1 * jnp.where(straight, g[1], g[2])
                til[j, rows, :] = jnp.where(straight, g[2], g[1])
        for i in range(height // SUB):
            at = FIRST + i * SUB
            rows = slice(i * SUB, (i + 1) * SUB)
            lanes = slice(j * LANES, (j + 1) * LANES)
            mob[j, at : at + SUB, :] = 0.1 * mobility[rows, lanes]
            til[j, at : at + SUB, :] = tilt[rows, lanes]
    place(a, FIRST, msg, 0, height // SUB)
    run_cycle(a, b, mob, til, drift, FIRST - RIM, FIRST + height + RIM)
    p[...] = a[:, FIRST - DEPTH : FIRST + height + DEPTH, :]


def off_kernel(msg, own_one, one, two, mob, til, drift, p, a, b):
    slab = lax.axis_index("space")
    low_end = slab == 0
    high_end = slab == lax.axis_size("space") - 1
    odd = slab % 2 == 1
    planes = a.shape[0]
    tiles = msg.shape[0] // planes
    height = tiles * SUB
    for ref in (a, b):
        blank(ref)
    for j in range(planes):
        for i in range(RIM // SUB):
            k = i * planes + j
            r = FIRST - RIM + i * SUB
            a[j, r : r + SUB, :] = jnp.where(low_end, own_one[0, k], jnp.where(odd, two[k], one[k]))
            r = FIRST + height + i * SUB
            a[j, r : r + SUB, :] = jnp.where(high_end, own_one[0, k], jnp.where(odd, one[k], two[k]))
    place(a, FIRST, msg, 0, tiles)
    run_cycle(a, b, mob, til, drift, FIRST - RIM, FIRST + height + RIM)
    p[...] = a[:, FIRST - DEPTH : FIRST + height + DEPTH, :]


def weights(msg):
    tile = msg[msg.shape[0] - 1]
    half = SUB // 2
    return jnp.broadcast_to(tile[0:1, :], tile.shape), jnp.broadcast_to(tile[half : half + 1, :], tile.shape)


def own_weights(msg):
    image = lax.axis_index("ladder")
    even = image % 2 == 0
    at_end = (image == 0) | (image == lax.axis_size("ladder") - 1)
    lower, upper = weights(msg)
    off = jnp.where(even, lower, upper)
    on = jnp.where(even, upper, lower)
    rest = 1.0 - lower - upper
    return jnp.where(at_end, rest + off, rest), jnp.where(at_end, 0.0, off), on


def off_weights(msg):
    even = lax.axis_index("ladder") % 2 == 0
    lower, upper = weights(msg)
    return 1.0 - lower - upper, jnp.where(even, upper, lower), jnp.where(even, lower, upper)


def second_kernel(which, msg, mid, one, two, mob, til, drift, q, a, b):
    planes, height, _ = q.shape
    for ref in (a, b):
        blank(ref)
    w = which(msg)
    for j in range(planes):
        for r in range(0, mid.shape[1], SUB):
            at = FIRST - DEPTH + r
            rows = slice(r, r + SUB)
            a[j, at : at + SUB, :] = w[0] * mid[j, rows, :] + w[1] * one[j, rows, :] + w[2] * two[j, rows, :]
    run_cycle(a, b, mob, til, drift, FIRST - DEPTH, FIRST + height + DEPTH)
    q[...] = a[:, FIRST : FIRST + height, :]


def blend_kernel(msg, mid, one, two, out):
    w = own_weights(msg)
    for j in range(mid.shape[0]):
        for r in range(0, mid.shape[1], SUB):
            rows = slice(r, r + SUB)
            out[rows, j * LANES : (j + 1) * LANES] = (
                w[0] * mid[j, rows, :] + w[1] * one[j, rows, :] + w[2] * two[j, rows, :]
            )


VMEM = pl.BlockSpec(memory_space=pltpu.VMEM)


def call(kernel, name, operands, shapes, scratch=(), ops=10**3):
    out = [jax.ShapeDtypeStruct(s, jnp.float32) for s in shapes]
    single = len(out) == 1
    return pl.pallas_call(
        kernel,
        out_shape=out[0] if single else out,
        in_specs=[VMEM] * len(operands),
        out_specs=VMEM if single else [VMEM] * len(out),
        scratch_shapes=[pltpu.VMEM(s, jnp.float32) for s in scratch],
        compiler_params=pltpu.CompilerParams(vmem_limit_bytes=6 * 2**20),
        cost_estimate=pl.CostEstimate(flops=ops, bytes_accessed=2**10, transcendentals=0),
        name=name,
    )(*operands)


def body(initial, mobility, tilt, drift, mix_weights):
    ladder = lax.axis_size("ladder")
    space = lax.axis_size("space")
    height, cols = initial.shape[1:]
    planes = cols // LANES
    work = (planes, height + 2 * RIM + 24, LANES)
    wide = (planes, height + 2 * DEPTH, LANES)
    slab = (planes, height, LANES)
    rim = (planes * RIM // SUB, SUB, LANES)

    def off(i):
        return (i - 1) % ladder if i % 2 == 0 else (i + 1) % ladder

    def beyond(i):
        return (i - 3) % ladder if i % 2 == 0 else (i + 3) % ladder

    swap_off = [(i, off(i)) for i in range(ladder)]
    swap_on = [(i, i ^ 1) for i in range(ladder)]
    swap_beyond = [(i, beyond(i)) for i in range(ladder)]
    both = ("ladder", "space")
    steps = [
        (i * space + s, i * space + s + 1 if s < space - 1 else off(i) * space, s)
        for i in range(ladder)
        for s in range(space)
    ]
    pairs_one = [q for a, b, s in steps if s % 2 == 1 for q in ((a, b), (b, a))]
    pairs_two = [q for a, b, s in steps if s % 2 == 0 for q in ((a, b), (b, a))]

    half = SUB // 2
    tiles = initial.reshape(height // SUB, SUB, planes, LANES).transpose(0, 2, 1, 3).reshape(-1, SUB, LANES)
    pair = jnp.broadcast_to(mix_weights.reshape(2, 1, 1), (2, half, LANES)).reshape(1, SUB, LANES)
    msg = jnp.concatenate([tiles, pair])
    other = lax.ppermute(msg, "ladder", swap_off)
    flow = drift.reshape(planes, LANES)

    one, two = call(edges_kernel, "edges", (msg, mobility, tilt), [(2, *rim)] * 2)
    own_one = lax.ppermute(one, both, pairs_one)
    own_two = lax.ppermute(two, both, pairs_two)
    one, two = call(off_edges_kernel, "off_edges", (other,), [rim] * 2, ops=4 * 10**10)
    one = lax.ppermute(one, both, pairs_one)
    two = lax.ppermute(two, both, pairs_two)
    one, two = lax.optimization_barrier((one, two))
    on_one = lax.ppermute(own_one[1], "ladder", swap_on)
    on_two = lax.ppermute(own_two[1], "ladder", swap_on)
    p_own, mob, til = call(
        own_kernel,
        "own_first",
        (msg, own_one, own_two, on_one, on_two, one, mobility, tilt, flow),
        [wide, work, work],
        [work, work],
        5 * 10**9,
    )
    p_on = lax.ppermute(p_own, "ladder", swap_on)
    p_off = call(off_kernel, "off_first", (other, own_one, one, two, mob, til, flow), [wide], [work, work], 5 * 10**9)
    p_beyond = lax.ppermute(p_off, "ladder", swap_beyond)

    q_own = call(
        functools.partial(second_kernel, own_weights),
        "own_second",
        (msg, p_own, p_off, p_on, mob, til, flow),
        [slab],
        [work, work],
        4 * 10**9,
    )
    q_on = lax.ppermute(q_own, "ladder", swap_on)
    q_off = call(
        functools.partial(second_kernel, off_weights),
        "off_second",
        (other, p_off, p_own, p_beyond, mob, til, flow),
        [slab],
        [work, work],
        4 * 10**9,
    )
    path = call(blend_kernel, "blend", (msg, q_own, q_off, q_on), [(height, cols)])
    return path[None]


def solution(mesh):
    in_specs = (
        P("ladder", "space", None),
        P("space", None),
        P("space", None),
        P(),
        P("ladder", None),
    )
    out_specs = P("ladder", "space", None)
    return jax.shard_map(body, mesh=mesh, in_specs=in_specs, out_specs=out_specs, check_vma=False)
```

```python
import functools

import jax
import jax.numpy as jnp
from jax import lax
from jax.experimental import pallas as pl
from jax.experimental.pallas import tpu as pltpu
from jax.sharding import PartitionSpec as P

DEPTH = 12
RIM = 2 * DEPTH
LANES = 128
SUB = 8
GROUP = 4
FIRST = 36


def spans(k, begin, end):
    return (begin + k) // SUB, -(-(end - k) // SUB)


def sweep(src, dst, mob, tilt, drift, span):
    planes = src.shape[0]
    lane = lax.broadcasted_iota(jnp.int32, (SUB, LANES), 1)
    is_first = lane == 0
    is_last = lane == LANES - 1
    for begin in range(0, planes, GROUP):
        group = range(begin, begin + GROUP)
        drifts = [jnp.broadcast_to(drift[j : j + 1, :], (SUB, LANES)) for j in group]
        rising = [u > 0 for u in drifts]
        speed = [jnp.abs(u) for u in drifts]
        for i in range(*span):
            r = i * SUB
            fields = [src[(begin - 1 + n) % planes, r : r + SUB, :] for n in range(GROUP + 2)]
            for n, j in enumerate(group):
                f = fields[n + 1]
                below = src[j, r - 1 : r - 1 + SUB, :]
                above = src[j, r + 1 : r + 1 + SUB, :]
                west = pltpu.roll(jnp.where(is_last, fields[n], f), 1, 1)
                east = pltpu.roll(jnp.where(is_first, fields[n + 2], f), LANES - 1, 1)
                near = (west + east) + (below + above)
                m = mob[j, r : r + SUB, :]
                t = tilt[j, r : r + SUB, :]
                gain = m * ((near + t) - f * (f * f + 3.0))
                dst[j, r : r + SUB, :] = (f + gain) + speed[n] * (jnp.where(rising[n], below, above) - f)


def run_cycle(a, b, mob, tilt, drift, begin, end):
    k = 1
    while k <= DEPTH:
        span = spans(k, begin, end)
        last = k
        while last < DEPTH and spans(last + 1, begin, end) == span:
            last += 1
        if k % 2 == 0:
            sweep(b, a, mob, tilt, drift, span)
            k += 1
            continue
        pairs = (last - k + 1) // 2
        if pairs:

            @pl.loop(0, pairs)
            def _(_):
                sweep(a, b, mob, tilt, drift, span)
                sweep(b, a, mob, tilt, drift, span)

            k += 2 * pairs
        else:
            sweep(a, b, mob, tilt, drift, span)
            k += 1


def place(dst, at, tiles, first, count):
    planes = dst.shape[0]
    for j in range(planes):
        for i in range(count):
            r = at + i * SUB
            dst[j, r : r + SUB, :] = tiles[(first + i) * planes + j]


def blank(ref):
    planes, rows, _ = ref.shape
    for j in range(planes):
        ref[j, 0:16, :] = jnp.zeros((16, LANES), jnp.float32)
        ref[j, rows - 16 : rows, :] = jnp.zeros((16, LANES), jnp.float32)


def pack_kernel(field, pair, msg):
    planes = field.shape[1] // LANES
    half = SUB // 2
    for i in range(field.shape[0] // SUB):
        for j in range(planes):
            msg[i * planes + j] = field[i * SUB : (i + 1) * SUB, j * LANES : (j + 1) * LANES]
    lower = jnp.broadcast_to(pair[0:1, 0:1], (SUB, LANES))
    upper = jnp.broadcast_to(pair[0:1, 1:2], (SUB, LANES))
    row = lax.broadcasted_iota(jnp.int32, (SUB, LANES), 0)
    msg[msg.shape[0] - 1] = jnp.where(row < half, lower, upper)


def edges_kernel(msg, mobility, tilt, one, two):
    odd = lax.axis_index("space") % 2 == 1
    even = lax.axis_index("ladder") % 2 == 0
    planes = mobility.shape[1] // LANES
    tiles = mobility.shape[0] // SUB
    count = RIM // SUB
    skip = tiles - count
    for i in range(count):
        for j in range(planes):
            k = i * planes + j
            lanes = slice(j * LANES, (j + 1) * LANES)
            lo = slice(i * SUB, (i + 1) * SUB)
            hi = slice((i + skip) * SUB, (i + skip + 1) * SUB)
            tops = msg[k + skip * planes], jnp.where(even, mobility[hi, lanes], tilt[hi, lanes])
            bottoms = msg[k], jnp.where(even, mobility[lo, lanes], tilt[lo, lanes])
            for n in range(2):
                one[n, k] = jnp.where(odd, tops[n], bottoms[n])
                two[n, k] = jnp.where(odd, bottoms[n], tops[n])


def off_edges_kernel(other, one, two):
    odd = lax.axis_index("space") % 2 == 1
    count = one.shape[0]
    skip = other.shape[0] - 1 - count
    for k in range(count):
        top = other[k + skip]
        bottom = other[k]
        one[k] = jnp.where(odd, top, bottom)
        two[k] = jnp.where(odd, bottom, top)


def own_kernel(msg, one, two, on_one, on_two, off_one, mobility, tilt, drift, p, mob, til, a, b):
    slab = lax.axis_index("space")
    low_end = slab == 0
    high_end = slab == lax.axis_size("space") - 1
    even = lax.axis_index("ladder") % 2 == 0
    odd = slab % 2 == 1
    height = mobility.shape[0]
    planes = a.shape[0]
    count = RIM // SUB
    for ref in (a, b, mob, til):
        blank(ref)
    for j in range(planes):
        for i in range(count):
            k = i * planes + j
            got = [(one[n, k], two[n, k]) for n in range(2)] + [(on_one[k], on_two[k])]
            lo = [jnp.where(odd, y, x) for x, y in got]
            hi = [jnp.where(odd, x, y) for x, y in got]
            for at, g, alone in ((FIRST - RIM, lo, low_end), (FIRST + height, hi, high_end)):
                rows = slice(at + i * SUB, at + (i + 1) * SUB)
                a[j, rows, :] = jnp.where(alone, off_one[k], g[0])
                straight = even != alone
                mob[j, rows, :] = 0.1 * jnp.where(straight, g[1], g[2])
                til[j, rows, :] = jnp.where(straight, g[2], g[1])
        for i in range(height // SUB):
            at = FIRST + i * SUB
            rows = slice(i * SUB, (i + 1) * SUB)
            lanes = slice(j * LANES, (j + 1) * LANES)
            mob[j, at : at + SUB, :] = 0.1 * mobility[rows, lanes]
            til[j, at : at + SUB, :] = tilt[rows, lanes]
    place(a, FIRST, msg, 0, height // SUB)
    run_cycle(a, b, mob, til, drift, FIRST - RIM, FIRST + height + RIM)
    p[...] = a[:, FIRST - DEPTH : FIRST + height + DEPTH, :]


def off_kernel(msg, own_one, one, two, mob, til, drift, p, a, b):
    slab = lax.axis_index("space")
    low_end = slab == 0
    high_end = slab == lax.axis_size("space") - 1
    odd = slab % 2 == 1
    planes = a.shape[0]
    tiles = msg.shape[0] // planes
    height = tiles * SUB
    for ref in (a, b):
        blank(ref)
    for j in range(planes):
        for i in range(RIM // SUB):
            k = i * planes + j
            r = FIRST - RIM + i * SUB
            a[j, r : r + SUB, :] = jnp.where(low_end, own_one[0, k], jnp.where(odd, two[k], one[k]))
            r = FIRST + height + i * SUB
            a[j, r : r + SUB, :] = jnp.where(high_end, own_one[0, k], jnp.where(odd, one[k], two[k]))
    place(a, FIRST, msg, 0, tiles)
    run_cycle(a, b, mob, til, drift, FIRST - RIM, FIRST + height + RIM)
    p[...] = a[:, FIRST - DEPTH : FIRST + height + DEPTH, :]


def weights(msg):
    tile = msg[msg.shape[0] - 1]
    half = SUB // 2
    return jnp.broadcast_to(tile[0:1, :], tile.shape), jnp.broadcast_to(tile[half : half + 1, :], tile.shape)


def own_weights(msg):
    image = lax.axis_index("ladder")
    even = image % 2 == 0
    at_end = (image == 0) | (image == lax.axis_size("ladder") - 1)
    lower, upper = weights(msg)
    off = jnp.where(even, lower, upper)
    on = jnp.where(even, upper, lower)
    rest = 1.0 - lower - upper
    return jnp.where(at_end, rest + off, rest), jnp.where(at_end, 0.0, off), on


def off_weights(msg):
    even = lax.axis_index("ladder") % 2 == 0
    lower, upper = weights(msg)
    return 1.0 - lower - upper, jnp.where(even, upper, lower), jnp.where(even, lower, upper)


def second_kernel(which, msg, mid, one, two, mob, til, drift, q, a, b):
    planes, height, _ = q.shape
    for ref in (a, b):
        blank(ref)
    w = which(msg)
    for j in range(planes):
        for r in range(0, mid.shape[1], SUB):
            at = FIRST - DEPTH + r
            rows = slice(r, r + SUB)
            a[j, at : at + SUB, :] = w[0] * mid[j, rows, :] + w[1] * one[j, rows, :] + w[2] * two[j, rows, :]
    run_cycle(a, b, mob, til, drift, FIRST - DEPTH, FIRST + height + DEPTH)
    q[...] = a[:, FIRST : FIRST + height, :]


def blend_kernel(msg, mid, one, two, out):
    w = own_weights(msg)
    for j in range(mid.shape[0]):
        for r in range(0, mid.shape[1], SUB):
            rows = slice(r, r + SUB)
            out[rows, j * LANES : (j + 1) * LANES] = (
                w[0] * mid[j, rows, :] + w[1] * one[j, rows, :] + w[2] * two[j, rows, :]
            )


VMEM = pl.BlockSpec(memory_space=pltpu.VMEM)


def call(kernel, name, operands, shapes, scratch=(), ops=10**3):
    out = [jax.ShapeDtypeStruct(s, jnp.float32) for s in shapes]
    single = len(out) == 1
    return pl.pallas_call(
        kernel,
        out_shape=out[0] if single else out,
        in_specs=[VMEM] * len(operands),
        out_specs=VMEM if single else [VMEM] * len(out),
        scratch_shapes=[pltpu.VMEM(s, jnp.float32) for s in scratch],
        compiler_params=pltpu.CompilerParams(vmem_limit_bytes=6 * 2**20),
        cost_estimate=pl.CostEstimate(flops=ops, bytes_accessed=2**10, transcendentals=0),
        name=name,
    )(*operands)


def body(initial, mobility, tilt, drift, mix_weights):
    ladder = lax.axis_size("ladder")
    space = lax.axis_size("space")
    height, cols = initial.shape[1:]
    planes = cols // LANES
    work = (planes, height + 2 * RIM + 24, LANES)
    wide = (planes, height + 2 * DEPTH, LANES)
    slab = (planes, height, LANES)
    rim = (planes * RIM // SUB, SUB, LANES)

    def off(i):
        return (i - 1) % ladder if i % 2 == 0 else (i + 1) % ladder

    def beyond(i):
        return (i - 3) % ladder if i % 2 == 0 else (i + 3) % ladder

    swap_off = [(i, off(i)) for i in range(ladder)]
    swap_on = [(i, i ^ 1) for i in range(ladder)]
    swap_beyond = [(i, beyond(i)) for i in range(ladder)]
    both = ("ladder", "space")
    steps = [
        (i * space + s, i * space + s + 1 if s < space - 1 else off(i) * space, s)
        for i in range(ladder)
        for s in range(space)
    ]
    pairs_one = [q for a, b, s in steps if s % 2 == 1 for q in ((a, b), (b, a))]
    pairs_two = [q for a, b, s in steps if s % 2 == 0 for q in ((a, b), (b, a))]

    msg = call(pack_kernel, "pack", (initial[0], mix_weights), [(planes * height // SUB + 1, SUB, LANES)])
    other = lax.ppermute(msg, "ladder", swap_off)
    flow = drift.reshape(planes, LANES)

    one, two = call(edges_kernel, "edges", (msg, mobility, tilt), [(2, *rim)] * 2)
    own_one = lax.ppermute(one, both, pairs_one)
    own_two = lax.ppermute(two, both, pairs_two)
    one, two = call(off_edges_kernel, "off_edges", (other,), [rim] * 2, ops=4 * 10**10)
    one = lax.ppermute(one, both, pairs_one)
    two = lax.ppermute(two, both, pairs_two)
    one, two = lax.optimization_barrier((one, two))
    on_one = lax.ppermute(own_one[1], "ladder", swap_on)
    on_two = lax.ppermute(own_two[1], "ladder", swap_on)
    p_own, mob, til = call(
        own_kernel,
        "own_first",
        (msg, own_one, own_two, on_one, on_two, one, mobility, tilt, flow),
        [wide, work, work],
        [work, work],
        5 * 10**9,
    )
    p_on = lax.ppermute(p_own, "ladder", swap_on)
    p_off = call(off_kernel, "off_first", (other, own_one, one, two, mob, til, flow), [wide], [work, work], 5 * 10**9)
    p_beyond = lax.ppermute(p_off, "ladder", swap_beyond)

    q_own = call(
        functools.partial(second_kernel, own_weights),
        "own_second",
        (msg, p_own, p_off, p_on, mob, til, flow),
        [slab],
        [work, work],
        4 * 10**9,
    )
    q_on = lax.ppermute(q_own, "ladder", swap_on)
    q_off = call(
        functools.partial(second_kernel, off_weights),
        "off_second",
        (other, p_off, p_own, p_beyond, mob, til, flow),
        [slab],
        [work, work],
        4 * 10**9,
    )
    path = call(blend_kernel, "blend", (msg, q_own, q_off, q_on), [(height, cols)])
    return path[None]


def solution(mesh):
    in_specs = (
        P("ladder", "space", None),
        P("space", None),
        P("space", None),
        P(),
        P("ladder", None),
    )
    out_specs = P("ladder", "space", None)
    return jax.shard_map(body, mesh=mesh, in_specs=in_specs, out_specs=out_specs, check_vma=False)
```
